32 devices in a mesh: groups: 2 (over y), curve: 4 (over z), mp: 4 (over x, core).
Axes of the slice: x: 2, y: 2, z: 4, core: 2. Of those that a mesh axis runs over, the one named last changes fastest.
Arguments:
- points: bfloat16 [8192, 512], P(('groups', 'curve')), parts along dimension 0, may hold values from -6 to 6
- owner: int32 [8192, 1], P(('groups', 'curve')), parts along dimension 0, may hold values from 0 to 3; in each aligned block of 1024 rows (0 to 1023, 1024 to 2047, ...) at most 512 rows name the same one
- local_order: int32 [8, 1024], P(('groups', 'curve')), parts along dimension 0, may hold values from 0 to 1023, each once within a row
- codes: int32 [8192], P(('groups', 'curve')), parts along dimension 0, may hold values from 1 to 4096
- w_in: bfloat16 [512, 4, 1024], P(None, None, 'mp'), may hold values from -0.25 to 0.25
- w_bc: bfloat16 [512, 4, 64], replicated, may hold values from -0.25 to 0.25
- decay_rate: float32 [2, 16], replicated, may hold values from 0 to 1
- dt_scale: float32 [2, 16], replicated, may hold values from 0.02 to 0.2
- skip_gain: float32 [2, 16], replicated, may hold values from 0.5 to 2
- w_out: bfloat16 [2, 1024, 512], replicated, may hold values from -0.125 to 0.125
Outputs:
- mixed: bfloat16 [8192, 512], P(('groups', 'curve'), 'mp'), parts along dimension 0
The draws below stay inside these ranges and needn't reach their ends.
There are 2 independent parts, one for each index of `groups`. The reference program is written for one: setup_inputs(seed, part) draws one part's arguments, and reference() takes and returns one part's arrays. A program takes and returns all parts, laid end to end along the dimension named above; an argument that names none is the same for every part. Nothing has to cross between parts.
Inputs may be any that keep to these rules, and one draw needn't show every extreme that they name: Among the points of one device no owner is named by more than 512. `local_order`: each row lists the points of one device in curve order, each once.
All inputs are finite; a program needn't handle non-finite values.
Results may differ from the reference program's by a relative error of at most 0.02.
Values may be sent and summed in bfloat16 or wider, within the bound.
A program may use at most 128 MiB of HBM per device.

```python
import math
import jax
import jax.numpy as jnp
import numpy as np
from jax import lax

D = 512
HEADS = 16
HEADDIM = 64
STATE = 64
PTS_DEV = 1024
DI = 1024
TOTAL = 4096
CAP = 512
N_CURVE = 4
N_MP = 4


def draw_codes(key, part):
    first, second, third = jax.random.split(key, 3)
    base = jax.random.randint(first, (TOTAL,), 1, 3)
    factor = jax.random.randint(second, (TOTAL // PTS_DEV,), 1, 3)
    codes = base * jnp.repeat(factor, PTS_DEV, total_repeat_length=TOTAL)
    spots = jax.random.randint(third, (2,), 0, TOTAL)
    codes = codes.at[spots].set(TOTAL)
    return codes.astype(jnp.int32)


def draw_decay_rate(key, part):
    first, second, third = jax.random.split(key, 3)
    slow_lo = jnp.log(0.22 / TOTAL)
    slow_hi = jnp.log(0.45 / TOTAL)
    fast_lo = jnp.log(0.008)
    fast_hi = jnp.log(0.02)
    slow = jnp.exp(slow_lo + jax.random.uniform(first, (2, HEADS), jnp.float32) * (slow_hi - slow_lo))
    fast = jnp.exp(fast_lo + jax.random.uniform(second, (2, HEADS), jnp.float32) * (fast_hi - fast_lo))
    picks = jax.random.randint(third, (2, HEADS), 0, 10)
    chosen = picks < 5
    return jnp.where(chosen, slow, fast).astype(jnp.float32)


def levels(own_key, extent, shards, low, high):
    loudness, own = 1.0, jax.random.fold_in(own_key, 6)
    for position, shards_of in shards:
        heights = jnp.exp(jax.random.uniform(jax.random.fold_in(own, position), (shards_of,), jnp.float32, low / len(shards), high / len(shards)))
        loudness = loudness * jnp.repeat(heights, extent[position] // shards_of).reshape([-1 if axis == position else 1 for axis in range(len(extent))])
    return loudness


def assign_block(stream_key, own, number, rows, amount, top, bound, skew):
    order = jax.random.permutation(stream_key, amount)
    packed, usual = portions_of(amount, rows * top, bound, skew, True), portions_of(amount, rows * top, bound, skew, False)
    places = jnp.arange(amount)

    def named(lengths, offset_by):
        used = int((lengths > 0).sum())
        fixed = max(1, used // 4)
        passed = fixed + (places - fixed + offset_by * (used - fixed)) % max(1, amount - fixed)
        return jnp.zeros((amount,), jnp.int32).at[order[jnp.where(places < fixed, places, passed)]].set(jnp.asarray(lengths, jnp.int32))

    lengths = jnp.where(number % 4 == 0, named(packed, number // 4), named(usual, number - number // 4 - 1))
    mixed = jax.random.permutation(jax.random.fold_in(own, 3), amount)
    source_of, receiver = mixed[0:amount // 2 * 2:2], mixed[1:amount // 2 * 2:2]
    slack = jnp.minimum(lengths[source_of] - 1, bound - lengths[receiver]) // 2
    slack = jnp.where((source_of == order[0]) | (receiver == order[0]) | (lengths[receiver] == 0), 0, jnp.maximum(slack, 0))
    passed = jax.random.randint(jax.random.fold_in(own, 4), (amount // 2,), 0, 1 << 20) % (slack + 1)
    lengths = lengths.at[source_of].add(-passed).at[receiver].add(passed)
    members = jnp.searchsorted(jnp.cumsum(lengths), jnp.arange(rows * top), side="right").astype(jnp.int32)
    table = members.reshape(top, rows).T
    table = table[jax.random.permutation(jax.random.fold_in(own, 1), rows)]
    offset_by = jax.random.randint(jax.random.fold_in(own, 2), (rows, 1), 0, top)
    return jnp.take_along_axis(table, (jnp.arange(top)[None, :] + offset_by) % top, axis=1)


def portions_of(count, total, most, slope, full):
    weights = [(1 << 20) // math.isqrt(grade ** slope) + 1 for grade in range(1, count + 1)]
    largest = most if full else min(most, max(-(-total // count), total * weights[0] // sum(weights)))
    least = 1 if total - largest >= count - 1 else 0
    given, spare = [largest] + [least] * (count - 1), total - largest - least * (count - 1)
    while spare > 0:
        movable = [i for i in range(1, count) if given[i] < largest] or [i for i in range(1, count) if given[i] < most]
        pool, remaining = sum([weights[i] for i in movable]), spare
        for i in movable:
            more = min(most - given[i], max(1, remaining * weights[i] // pool), spare)
            given[i] = given[i] + more
            spare = spare - more
    return np.array(given)


def normal_values(rng, shape, width, reach, pieces=(), held_as=jnp.bfloat16):
    factor_of = levels(rng, shape, pieces, -0.22, 0.18) if pieces else 1.0
    entries = jax.random.normal(rng, shape, jnp.float32) * width * factor_of
    return jnp.minimum(jnp.maximum(entries, -reach), reach).astype(held_as)


def setup_inputs(seed: int = 0, part: int = 0) -> dict:
    seeds = jax.random.split(jax.random.key(seed), 11)
    part_keys = jax.random.split(jax.random.fold_in(seeds[10], part), 11)
    points = normal_values(part_keys[0], (TOTAL, D), 1.0, 6.0, ((0, 4),))
    owner_keys = jax.random.split(jax.random.fold_in(part_keys[1], 1), TOTAL // PTS_DEV)
    owner_turns = jax.random.permutation(jax.random.fold_in(part_keys[1], 3), TOTAL // PTS_DEV)
    owner = jax.vmap(lambda own, number: assign_block(jax.random.fold_in(part_keys[1], 2), own, number, PTS_DEV, N_CURVE, 1, CAP, 2))(owner_keys, owner_turns).reshape((TOTAL, 1))
    local_order = jax.vmap(lambda own: jax.random.permutation(own, PTS_DEV))(jax.random.split(part_keys[2], N_CURVE)).reshape((N_CURVE, PTS_DEV)).astype(jnp.int32)
    codes = draw_codes(jax.random.fold_in(jax.random.fold_in(seeds[10], part), 71), part)
    w_in = normal_values(seeds[4], (D, 4, DI), D ** -0.5, 0.25, ((2, 4),))
    w_bc = normal_values(seeds[5], (D, 4, STATE), D ** -0.5, 0.25)
    decay_rate = draw_decay_rate(jax.random.fold_in(seeds[10], 71), part)
    dt_scale = jnp.clip(jnp.exp(jax.random.uniform(seeds[7], (2, HEADS), jnp.float32, math.log(0.02), math.log(0.2))), 0.02, 0.2)
    skip_gain = jnp.clip(jax.random.uniform(seeds[8], (2, HEADS), jnp.float32, 0.5, 2.0), 0.5, 2.0)
    w_out = normal_values(seeds[9], (2, DI, D), (2 * DI) ** -0.5, 0.125)
    return {"points": points, "owner": owner, "local_order": local_order, "codes": codes, "w_in": w_in, "w_bc": w_bc, "decay_rate": decay_rate, "dt_scale": dt_scale, "skip_gain": skip_gain, "w_out": w_out}


def sweep(inputs, keys, queries, logs):

    def step(state, item):
        u, b, c, l = item
        state = jnp.exp(l)[:, None, None] * state + b[None, :, None] * u[:, None, :]
        out = jnp.einsum('n,hnp->hp', c, state, precision=lax.Precision.HIGHEST)
        return (state, out)
    start = jnp.zeros((HEADS, STATE, HEADDIM), jnp.float32)
    final, outs = lax.scan(step, start, (inputs, keys, queries, logs))
    return outs

def reference(points, owner, local_order, codes, w_in, w_bc, decay_rate, dt_scale, skip_gain, w_out):
    source = jnp.arange(TOTAL, dtype=jnp.int32) // PTS_DEV
    where_at = (jnp.arange(N_CURVE, dtype=jnp.int32)[:, None] * PTS_DEV + local_order).reshape(-1)
    rank = jnp.zeros((TOTAL,), jnp.int32).at[where_at].set(jnp.tile(jnp.arange(PTS_DEV, dtype=jnp.int32), N_CURVE))
    sort_key = owner[:, 0] * TOTAL + source * PTS_DEV + rank
    perm = jnp.argsort(sort_key).astype(jnp.int32)
    seq = points[perm]
    code = codes[perm].astype(jnp.float32)
    proj = jnp.dot(seq, w_in.reshape(D, 4 * DI), preferred_element_type=jnp.float32).astype(jnp.bfloat16)
    proj = lax.optimization_barrier(proj).astype(jnp.float32).reshape(TOTAL, 4, DI)
    bc = jnp.dot(seq, w_bc.reshape(D, 4 * STATE), preferred_element_type=jnp.float32).astype(jnp.bfloat16)
    bc = lax.optimization_barrier(bc).astype(jnp.float32).reshape(TOTAL, 4, STATE)
    normed = []
    for direction in range(2):
        xh = proj[:, 2 * direction].reshape(TOTAL, HEADS, HEADDIM)
        gate = proj[:, 2 * direction + 1].reshape(TOTAL, HEADS, HEADDIM)
        keys = bc[:, 2 * direction]
        queries = bc[:, 2 * direction + 1]
        logs = -decay_rate[direction][None, :] * code[:, None]
        inputs = xh * dt_scale[direction][None, :, None]
        if direction == 1:
            outs = jnp.flip(sweep(jnp.flip(inputs, 0), jnp.flip(keys, 0), jnp.flip(queries, 0), jnp.flip(logs, 0)), 0)
        else:
            outs = sweep(inputs, keys, queries, logs)
        outs = outs + skip_gain[direction][None, :, None] * xh
        value = outs * jax.nn.silu(gate)
        value = value / jnp.sqrt(lax.optimization_barrier(jnp.mean(value * value, axis=-1, keepdims=True)) + 1e-05)
        normed.append(value.astype(jnp.bfloat16))
    heads_local = HEADS // N_MP
    width_local = heads_local * HEADDIM
    total = jnp.zeros((TOTAL, D), jnp.float32)
    for group in range(N_MP):
        piece = jnp.stack([normed[0][:, group * heads_local:(group + 1) * heads_local].reshape(TOTAL, width_local), normed[1][:, group * heads_local:(group + 1) * heads_local].reshape(TOTAL, width_local)], axis=1)
        rows_w = w_out[:, group * width_local:(group + 1) * width_local, :].reshape(2 * width_local, D)
        partial_sum = jnp.dot(piece.reshape(TOTAL, 2 * width_local), rows_w, preferred_element_type=jnp.float32)
        partial_sum = lax.optimization_barrier(partial_sum.astype(jnp.bfloat16)).astype(jnp.float32)
        total = total + partial_sum
    out_seq = total.astype(jnp.bfloat16)
    return jnp.zeros((TOTAL, D), jnp.bfloat16).at[perm].set(out_seq)
```

```python
import functools

import jax
import jax.numpy as jnp
from jax import lax
from jax.experimental import pallas as pl
from jax.experimental.pallas import tpu as pltpu
from jax.sharding import PartitionSpec as P

HEADS = 16
HEADDIM = 64
SPAN = 256
LOG2E = 1.4426950408889634
F32 = jnp.float32
BF16 = jnp.bfloat16
MESH = pl.DeviceIdType.MESH


def running(a, axis):
    size = a.shape[axis]
    lower = (jnp.arange(size)[:, None] >= jnp.arange(size)[None, :]).astype(F32)
    moved = jnp.tensordot(lower, a.astype(F32), axes=(1, axis), precision=lax.Precision.HIGHEST)
    return jnp.moveaxis(moved, 0, axis)


def prefix(value, axis, combine, identity, reverse):
    peers, place = (lax.axis_size(axis), lax.axis_index(axis))
    everything = jax.tree.map(
        lambda part, kind: lax.all_gather(part.astype(kind), axis),
        value,
        jax.tree.map(lambda a: jnp.bfloat16 if a.dtype == jnp.float32 else a.dtype, value),
    )
    start = jax.tree.map(
        lambda part, zero: jnp.broadcast_to(jnp.asarray(zero, part.dtype), part.shape),
        value,
        identity,
    )

    def lap(k, before):
        at = peers - 1 - k if reverse else k
        reached = at > place if reverse else at < place
        new = combine(
            before, jax.tree.map(lambda part, own: part[at].astype(own.dtype), everything, value)
        )
        return jax.tree.map(lambda a, b: jnp.where(reached, a, b), new, before)

    return lax.fori_loop(0, peers, lap, start)


def local_pass(inputs, keys, queries, logs):
    rows, heads_local, width = inputs.shape
    blocks = rows // SPAN
    xblock = inputs.reshape(blocks, SPAN, heads_local, width)
    kblock_low = keys.reshape(blocks, SPAN, keys.shape[1])
    qblock_low = queries.reshape(blocks, SPAN, queries.shape[1])
    kblock = kblock_low.astype(jnp.float32)
    qblock = qblock_low.astype(jnp.float32)
    lcum = running(logs.reshape(blocks, SPAN, heads_local), 1)
    scores = jnp.einsum("cqn,csn->cqs", qblock_low, kblock_low, preferred_element_type=jnp.float32)
    causal = jnp.arange(SPAN)[:, None] >= jnp.arange(SPAN)[None, :]
    gap = lcum[:, :, None, :] - lcum[:, None, :, :]
    weight = jnp.where(
        causal[None, :, :, None], jnp.exp(jnp.where(causal[None, :, :, None], gap, 0.0)), 0.0
    )
    intra = jnp.einsum(
        "cqsh,cshp->cqhp", scores[..., None] * weight, xblock, precision=lax.Precision.HIGHEST
    )
    tail = jnp.exp(lcum[:, -1:, :] - lcum)
    block_state = jnp.einsum(
        "csn,cshp->chnp", kblock, xblock * tail[..., None], precision=lax.Precision.HIGHEST
    )
    block_log = lcum[:, -1, :]

    def advance(state, item):
        log_c, new_state = item
        return (jnp.exp(log_c)[:, None, None] * state + new_state, state)

    start = jnp.zeros((heads_local, keys.shape[1], width), jnp.float32)
    final, entering = lax.scan(advance, start, (block_log, block_state))
    total_log = jnp.sum(block_log, axis=0)
    return ((qblock, lcum, intra, entering, block_log), (total_log, final))


def finish(pieces, carried):
    qblock, lcum, intra, entering, block_log = pieces
    before = running(block_log, 0) - block_log
    enter_all = entering + jnp.exp(before)[:, :, None, None] * carried[None]
    inter = jnp.exp(lcum)[..., None] * jnp.einsum(
        "cqn,chnp->cqhp", qblock, enter_all, precision=lax.Precision.HIGHEST
    )
    total = intra + inter
    return total.reshape(-1, total.shape[2], total.shape[3])


def combine(earlier, later):
    return (earlier[0] + later[0], jnp.exp(later[0])[:, None, None] * earlier[1] + later[1])


def per_device(
    points, owner, local_order, codes, w_in, w_bc, decay_rate, dt_scale, skip_gain, w_out
):
    n_curve = lax.axis_size("curve")
    n_model = lax.axis_size("mp")
    count = points.shape[0]
    rows = 2 * count
    slots = rows // n_curve
    heads_local = HEADS // n_model
    model_index = lax.axis_index("mp")
    order = local_order[0]
    sorted_owner = owner[:, 0][order]
    onehot = (sorted_owner[:, None] == jnp.arange(n_curve, dtype=jnp.int32)[None, :]).astype(
        jnp.int32
    )
    slot = jnp.sum(running(onehot, 0) * onehot, axis=1).astype(jnp.int32) - 1
    target = jnp.zeros((count,), jnp.int32).at[order].set(sorted_owner * slots + slot)
    send_codes = jnp.zeros((rows,), jnp.int32).at[target].set(codes)
    send_rows = jnp.zeros((rows, points.shape[1]), points.dtype).at[target].set(points)
    arrived, arrived_codes = (
        lax.all_to_all(send_rows, "curve", split_axis=0, concat_axis=0, tiled=True),
        lax.all_to_all(send_codes, "curve", split_axis=0, concat_axis=0, tiled=True),
    )
    proj_sum = jnp.einsum("rk,kjc->rjc", arrived, w_in, preferred_element_type=jnp.float32)
    bc_sum = jnp.einsum("rk,kjc->rjc", arrived, w_bc, preferred_element_type=jnp.float32)
    proj = lax.optimization_barrier(proj_sum.astype(jnp.bfloat16)).astype(jnp.float32)
    bc = bc_sum.astype(jnp.bfloat16)
    code_f = arrived_codes.astype(jnp.float32)
    rates = lax.dynamic_slice_in_dim(decay_rate, model_index * heads_local, heads_local, 1)
    steps_dt = lax.dynamic_slice_in_dim(dt_scale, model_index * heads_local, heads_local, 1)
    skips = lax.dynamic_slice_in_dim(skip_gain, model_index * heads_local, heads_local, 1)
    pieces = []
    summaries = []
    xparts = []
    gates = []
    for direction in range(2):
        xh = proj[:, 2 * direction].reshape(rows, heads_local, HEADDIM)
        gates.append(proj[:, 2 * direction + 1].reshape(rows, heads_local, HEADDIM))
        xparts.append(xh)
        inputs = xh * steps_dt[direction][None, :, None]
        keys = bc[:, 2 * direction]
        queries = bc[:, 2 * direction + 1]
        logs = -rates[direction][None, :] * code_f[:, None]
        if direction == 1:
            inputs, keys, queries, logs = (
                jnp.flip(inputs, 0),
                jnp.flip(keys, 0),
                jnp.flip(queries, 0),
                jnp.flip(logs, 0),
            )
        kept, summary = local_pass(inputs, keys, queries, logs)
        pieces.append(kept)
        summaries.append(summary)
    ident = (jnp.zeros((heads_local,), jnp.float32), jnp.zeros_like(summaries[0][1]))
    forward_in = prefix(summaries[0], "curve", combine, ident, False)[1]
    backward_in = prefix(summaries[1], "curve", combine, ident, True)[1]
    carried_all = (forward_in, backward_in)
    normed = []
    for direction in range(2):
        outs = finish(pieces[direction], carried_all[direction])
        if direction == 1:
            outs = jnp.flip(outs, 0)
        outs = outs + skips[direction][None, :, None] * xparts[direction]
        value = outs * jax.nn.silu(gates[direction])
        value = value / jnp.sqrt(jnp.mean(value * value, axis=-1, keepdims=True) + 1e-05)
        normed.append(value.astype(jnp.bfloat16).reshape(rows, heads_local * HEADDIM))
    stacked = jnp.stack(normed, axis=1)
    w_rows = lax.dynamic_slice_in_dim(
        w_out, model_index * heads_local * HEADDIM, heads_local * HEADDIM, 1
    )
    terms = jnp.einsum("rdk,dkc->rc", stacked, w_rows, preferred_element_type=jnp.float32)
    summed = lax.psum_scatter(terms.astype(jnp.bfloat16), "mp", scatter_dimension=1, tiled=True)
    back = lax.all_to_all(summed, "curve", split_axis=0, concat_axis=0, tiled=True)
    return back[target]


def mm(a, b, ca=1, cb=0):
    return lax.dot_general(a, b, (((ca,), (cb,)), ((), ())), preferred_element_type=F32)


def iota(shape, dim):
    return lax.broadcasted_iota(jnp.int32, shape, dim)


def as_bf16(mask):
    return jnp.where(mask, 1.0, 0.0).astype(BF16)


def layer_kernel(
    nc,
    slots,
    pts,
    own,
    order,
    codes,
    w,
    rate_lane,
    dt_lane,
    skip_lane,
    rate,
    wo,
    out,
    sendb,
    tt,
    csend,
    carr,
    arr,
    proj,
    cols,
    rowv,
    ctot,
    cst,
    ent,
    pre,
    ssend,
    srecv,
    dsend,
    drecv,
    carried,
    part,
    recva,
    sendx,
    recvx,
    sumc,
    back,
    zs,
    zr,
    cs,
    cr,
    xs,
    xr,
    ps,
    pr,
    fs,
    fr,
    ss,
    sr,
    ds,
    dr,
    gs,
    gr,
    hs,
    hr,
    bs,
    br,
):
    count = pts.shape[0]
    share = slots // 4
    halves = slots // SPAN
    chunks = nc * halves
    me = lax.axis_index("curve")
    q = lax.axis_index("mp")
    core = lax.rem(q, 2)
    xx = lax.div(q, 2)
    other_core = q + 1 - 2 * core
    other_x = q + 2 - 4 * xx
    to_core = {"mp": other_core}
    to_x = {"mp": other_x}

    def after(k):
        return lax.rem(me + k, nc)

    def before(k):
        return lax.rem(me - k + nc, nc)

    def copy(src, dst, s, r, where):
        return pltpu.make_async_remote_copy(
            src_ref=src, dst_ref=dst, send_sem=s, recv_sem=r, device_id=where, device_id_type=MESH
        )

    def at(start, size):
        return pl.ds(pl.multiple_of(start, size), size)

    barrier = pltpu.get_barrier_semaphore()
    for k in range(1, nc):
        pl.semaphore_signal(barrier, inc=1, device_id={"curve": after(k)}, device_id_type=MESH)
    for there in (to_core, to_x):
        pl.semaphore_signal(barrier, inc=1, device_id=there, device_id_type=MESH)

    picks = as_bf16(iota((count, count), 0) == order[...])
    own8 = jnp.broadcast_to(own[...].astype(F32), (8, count)).astype(BF16)
    sorted8 = mm(own8, picks)
    hot8 = as_bf16(sorted8 == iota((8, count), 0).astype(F32))
    upper = as_bf16(iota((count, count), 0) <= iota((count, count), 1))
    counts = mm(hot8, upper)
    slot = jnp.sum(counts * hot8.astype(F32), axis=0, keepdims=True) - 1.0
    target = sorted8[0:1] * float(slots) + slot
    high = jnp.floor(target * (1.0 / 64.0))
    low = target - high * 64.0
    split8 = jnp.where(iota((8, count), 0) == 0, high, low).astype(BF16)
    trow8 = mm(split8, picks, 1, 1)
    trow = trow8[0:1] * 64.0 + trow8[1:2]
    tcol8 = mm(picks, split8, 1, 1)
    tcol = tcol8[:, 0:1] * 64.0 + tcol8[:, 1:2]

    def routed(t):
        place = (iota((share, count), 0) + (t * slots + q * share)).astype(F32)
        return mm(as_bf16(place == trow), pts[...]).astype(BF16)

    def zcopy(k):
        return copy(
            sendb.at[k],
            arr.at[at(me * slots + q * share, share)],
            zs.at[k],
            zr.at[k],
            {"curve": after(k)},
        )

    def ccopy(k):
        return copy(csend.at[after(k)], carr.at[me], cs.at[k], cr.at[k], {"curve": after(k)})

    def mine(s, who):
        return arr.at[at(s * slots + who * share, share)]

    def xcopy(k):
        s = before(k)
        return copy(mine(s, q), mine(s, q), xs.at[k], xr.at[k], to_x)

    def pcopy(k):
        s = before(k)
        return copy(mine(s, q), mine(s, q), ps.at[k], pr.at[k], to_core)

    def fcopy(k):
        s = before(k)
        return copy(mine(s, other_x), mine(s, other_x), fs.at[k], fr.at[k], to_core)

    first = routed(after(nc - 1))
    sendb[nc - 1] = first
    pl.semaphore_wait(barrier, nc + 1)
    zcopy(nc - 1).start()
    for k in range(nc - 2, 0, -1):
        sendb[k] = routed(after(k))
        zcopy(k).start()
    arr[at(me * slots + q * share, share)] = routed(me)
    xcopy(0).start()
    pcopy(0).start()

    codef = codes[...].astype(F32)
    chigh = jnp.floor(codef * (1.0 / 128.0))
    code8 = jnp.where(iota((8, count), 0) == 0, chigh, codef - chigh * 128.0).astype(BF16)
    for t in range(nc):
        hot = as_bf16(tcol == (iota((count, slots), 1) + t * slots).astype(F32))
        tt[t] = hot
        made = mm(code8, hot)
        for h in range(halves):
            csend[t, h] = made[:, h * SPAN : (h + 1) * SPAN]
    for k in range(1, nc):
        ccopy(k).start()
    carr[me] = csend[me]

    above = iota((SPAN, SPAN), 0) <= iota((SPAN, SPAN), 1)
    below = iota((SPAN, SPAN), 0) >= iota((SPAN, SPAN), 1)

    def project(s):
        def half(h, _):
            c = s * halves + h
            rows = at(c * SPAN, SPAN)
            made = mm(arr[rows, :], w[...]).astype(BF16)
            proj[rows, :] = made
            c8 = carr[s, h].astype(BF16)
            run8 = mm(c8, as_bf16(above))
            srow = run8[0:1] * 128.0 + run8[1:2]
            own_row = carr[s, h]
            erow = srow - (own_row[0:1] * 128.0 + own_row[1:2])
            rowv[c, 0:1, :] = srow
            rowv[c, 1:2, :] = erow
            scol8 = mm(as_bf16(below), c8, 1, 1)
            scol = scol8[:, 0:1] * 128.0 + scol8[:, 1:2]
            strict = as_bf16(iota((SPAN, SPAN), 0) > iota((SPAN, SPAN), 1))
            ecol8 = mm(strict, c8, 1, 1)
            ecol = ecol8[:, 0:1] * 128.0 + ecol8[:, 1:2]
            cols[0, rows, :] = jnp.broadcast_to(scol, (SPAN, 128))
            cols[1, rows, :] = jnp.broadcast_to(ecol, (SPAN, 128))
            total = srow[:, SPAN - 1 : SPAN]
            ctot[c] = jnp.broadcast_to(total, (8, 256))
            for d, reach in ((0, scol - total), (1, -ecol)):
                tail = jnp.exp2(rate_lane[d] * reach)
                xt = (made[:, 512 * d : 512 * d + 256].astype(F32) * tail).astype(BF16)
                keys = made[:, 1024 + 256 * d : 1152 + 256 * d]
                cst[d, c] = mm(keys, xt, 0, 0)[0:64]
            return 0

        lax.fori_loop(0, halves, half, 0)

    def complete(k):
        pcopy(k).wait_recv()
        fcopy(k).wait_recv()
        if k:
            ccopy(k).wait_recv()
        project(before(k))

    xcopy(0).wait_recv()
    fcopy(0).start()
    for k in range(1, nc):
        zcopy(k).wait_recv()
        xcopy(k).start()
        pcopy(k).start()
        complete(k - 1)
        xcopy(k).wait_recv()
        fcopy(k).start()
    complete(nc - 1)

    for d in range(2):
        state = jnp.zeros((64, 256), F32)
        passed = jnp.zeros((8, 256), F32)
        for step in range(chunks):
            c = step if d == 0 else chunks - 1 - step
            ent[d, c] = state
            pre[d, c] = passed
            gone = ctot[c]
            state = jnp.exp2(-rate_lane[d] * gone[0:1]) * state + cst[d, c]
            passed = passed + gone
        ssend[d] = state.astype(BF16)
        dsend[...] = passed

    def scopy(k):
        t = after(k)
        which = jnp.where(t > me, 0, 1)
        return copy(ssend.at[which], srecv.at[k], ss.at[k], sr.at[k], {"curve": t})

    def dcopy(k):
        return copy(dsend, drecv.at[k], ds.at[k], dr.at[k], {"curve": after(k)})

    for k in range(1, nc):
        scopy(k).start()
        dcopy(k).start()
    for k in range(1, nc):
        scopy(k).wait_recv()
        dcopy(k).wait_recv()
    for d in range(2):
        total = jnp.zeros((64, 256), F32)
        for k in range(1, nc):
            s = before(k)
            gap = jnp.zeros((1, 256), F32)
            for j in range(1, nc):
                u = before(j)
                if d == 0:
                    inside = jnp.logical_and(u > s, u < me)
                else:
                    inside = jnp.logical_and(u < s, u > me)
                gap = gap + jnp.where(inside, drecv[j][0:1], 0.0)
            counted = (s < me) if d == 0 else (s > me)
            term = jnp.exp2(-rate_lane[d] * gap) * srecv[k].astype(F32)
            total = total + jnp.where(counted, term, 0.0)
        carried[d] = total

    def attend(c):
        rows = at(c * SPAN, SPAN)
        normed = []
        for d in range(2):
            x = proj[rows, 512 * d : 512 * d + 256]
            z = proj[rows, 512 * d + 256 : 512 * d + 512].astype(F32)
            keys = proj[rows, 1024 + 256 * d : 1152 + 256 * d]
            queries = proj[rows, 1152 + 256 * d : 1280 + 256 * d]
            scores = jnp.where(below if d == 0 else above, mm(queries, keys, 1, 1), 0.0)
            col = cols[d, rows, :]
            col = jnp.concatenate([col, col], axis=1)
            row = rowv[c, d : d + 1, :]
            gap = jnp.minimum((row - col) if d == 0 else (col - row), 0.0)
            pairs = []
            for p in range(2):
                xp = x[:, 128 * p : 128 * p + 128]
                left = iota((SPAN, 128), 1) < 64
                nothing = jnp.zeros_like(xp)
                weights = [
                    (scores * jnp.exp2(rate[d, 2 * p + h] * gap)).astype(BF16) for h in range(2)
                ]
                pairs.append(
                    mm(
                        jnp.concatenate(weights, axis=1),
                        jnp.concatenate(
                            [jnp.where(left, xp, nothing), jnp.where(left, nothing, xp)], axis=0
                        ),
                    )
                )
            intra = jnp.concatenate(pairs, axis=1)
            lanes = rate_lane[d]
            entering = ent[d, c] + jnp.exp2(-lanes * pre[d, c][0:1]) * carried[d]
            reach = -col if d == 0 else col - ctot[c][0:1]
            inter = mm(queries[:, 0:64], entering.astype(BF16)) * jnp.exp2(lanes * reach)
            y = dt_lane[d] * (intra + inter) + skip_lane[d] * x.astype(F32)
            v = y * (z / (1.0 + jnp.exp(-z)))
            same = as_bf16((iota((256, 256), 0) // 64) == (iota((256, 256), 1) // 64))
            mean = mm((v * v).astype(BF16), same) * (1.0 / 64.0)
            normed.append((v * lax.rsqrt(mean + 1e-05)).astype(BF16))
        terms = mm(jnp.concatenate(normed, axis=1), wo[...]).astype(BF16)
        for m in range(4):
            part[m % 2, m // 2, rows, :] = terms[:, 128 * m : 128 * m + 128]

    def rows_of(k):
        return at(after(k) * slots, slots)

    def acopy(k):
        rows = rows_of(k)
        return copy(part.at[1 - core, :, rows], recva.at[:, rows], gs.at[k], gr.at[k], to_core)

    def bcopy(k):
        rows = rows_of(k)
        return copy(sendx.at[rows], recvx.at[rows], hs.at[k], hr.at[k], to_x)

    def backcopy(k):
        return copy(
            sumc.at[rows_of(k)], back.at[at(me * slots, slots)], bs.at[k], br.at[k], {"curve": after(k)}
        )

    def cross(k):
        acopy(k).wait_recv()
        rows = rows_of(k)
        sendx[rows, :] = (
            part[core, 1 - xx, rows, :].astype(F32) + recva[1 - xx, rows, :].astype(F32)
        ).astype(BF16)
        bcopy(k).start()

    def home(k):
        bcopy(k).wait_recv()
        rows = rows_of(k)
        total = (
            part[core, xx, rows, :].astype(F32)
            + recva[xx, rows, :].astype(F32)
            + recvx[rows, :].astype(F32)
        ).astype(BF16)
        if k:
            sumc[rows, :] = total
            backcopy(k).start()
        else:
            back[rows, :] = total

    turns = list(range(nc - 1, -1, -1))
    for step in range(nc + 2):
        if step < nc:
            k = turns[step]

            def one(h, _, k=k):
                attend(after(k) * halves + h)
                return 0

            lax.fori_loop(0, halves, one, 0)
            acopy(k).start()
        if 1 <= step <= nc:
            cross(turns[step - 1])
        if 2 <= step:
            home(turns[step - 2])
    for k in range(1, nc):
        backcopy(k).wait_recv()
    total = jnp.zeros((count, 128), F32)
    for t in range(nc):
        total = total + mm(tt[t], back[t * slots : (t + 1) * slots, :])
    out[...] = total.astype(BF16)

    for k in range(nc):
        xcopy(k).wait_send()
        pcopy(k).wait_send()
        fcopy(k).wait_send()
        acopy(k).wait_send()
        bcopy(k).wait_send()
        if k:
            zcopy(k).wait_send()
            ccopy(k).wait_send()
            scopy(k).wait_send()
            dcopy(k).wait_send()
            backcopy(k).wait_send()


def fused_device(
    points, owner, local_order, codes, w_in, w_bc, decay_rate, dt_scale, skip_gain, w_out
):
    nc = lax.axis_size("curve")
    n_model = lax.axis_size("mp")
    count, width = points.shape
    rows = 2 * count
    slots = rows // nc
    halves = slots // SPAN
    chunks = nc * halves
    hl = HEADS // n_model
    cut = hl * HEADDIM
    m = lax.axis_index("mp")
    rates = lax.dynamic_slice_in_dim(decay_rate, m * hl, hl, 1) * LOG2E
    steps = lax.dynamic_slice_in_dim(dt_scale, m * hl, hl, 1)
    skips = lax.dynamic_slice_in_dim(skip_gain, m * hl, hl, 1)
    lanes = lambda a: jnp.repeat(a, HEADDIM, axis=1)[:, None, :]
    wbc = jnp.pad(w_bc, ((0, 0), (0, 0), (0, 64))).reshape(width, 512)
    w = jnp.concatenate([w_in.reshape(width, 4 * cut), wbc], axis=1)
    wo = lax.dynamic_slice_in_dim(w_out, m * cut, cut, 1).reshape(2 * cut, width)
    vm = pltpu.VMEM
    sem = pltpu.SemaphoreType.DMA
    vspec = pl.BlockSpec(memory_space=pltpu.VMEM)
    sspec = pl.BlockSpec(memory_space=pltpu.SMEM)
    return pl.pallas_call(
        functools.partial(layer_kernel, nc, slots),
        out_shape=jax.ShapeDtypeStruct((count, width // 4), BF16),
        in_specs=[vspec] * 8 + [sspec, vspec],
        out_specs=vspec,
        scratch_shapes=[
            vm((nc, slots // 4, width), BF16),
            vm((nc, count, slots), BF16),
            vm((nc, halves, 8, SPAN), F32),
            vm((nc, halves, 8, SPAN), F32),
            vm((rows, width), BF16),
            vm((rows, w.shape[1]), BF16),
            vm((2, rows, 128), F32),
            vm((chunks, 8, SPAN), F32),
            vm((chunks, 8, 256), F32),
            vm((2, chunks, 64, 256), F32),
            vm((2, chunks, 64, 256), F32),
            vm((2, chunks, 8, 256), F32),
            vm((2, 64, 256), BF16),
            vm((nc, 64, 256), BF16),
            vm((8, 256), F32),
            vm((nc, 8, 256), F32),
            vm((2, 64, 256), F32),
            vm((2, 2, rows, 128), BF16),
            vm((2, rows, 128), BF16),
            vm((rows, 128), BF16),
            vm((rows, 128), BF16),
            vm((rows, 128), BF16),
            vm((rows, 128), BF16),
        ]
        + [sem((nc,))] * 20,
        compiler_params=pltpu.CompilerParams(
            collective_id=0, has_side_effects=True, vmem_limit_bytes=56 * 1024 * 1024
        ),
    )(
        points,
        owner.reshape(1, count),
        local_order,
        codes.reshape(1, count),
        w,
        lanes(rates),
        lanes(steps),
        lanes(skips),
        rates,
        wo,
    )


def solution(mesh):
    placed = (
        P(("groups", "curve"), None),
        P(("groups", "curve"), None),
        P(("groups", "curve"), None),
        P(("groups", "curve")),
        P(None, None, "mp"),
        P(),
        P(),
        P(),
        P(),
        P(),
    )
    sizes = dict(mesh.shape)

    def body(points, *rest):
        slots = 2 * points.shape[0] // sizes["curve"]
        if sizes["mp"] == 4 and slots % SPAN == 0 and sizes["curve"] <= 8:
            return fused_device(points, *rest)
        return per_device(points, *rest)

    return jax.shard_map(
        body,
        mesh=mesh,
        in_specs=placed,
        out_specs=P(("groups", "curve"), "mp"),
        check_vma=False,
    )
```

```python
import functools

import jax
import jax.numpy as jnp
from jax import lax
from jax.experimental import pallas as pl
from jax.experimental.pallas import tpu as pltpu
from jax.sharding import PartitionSpec as P

HEADS = 16
HEADDIM = 64
SPAN = 256
LOG2E = 1.4426950408889634
F32 = jnp.float32
BF16 = jnp.bfloat16
MESH = pl.DeviceIdType.MESH


def running(a, axis):
    size = a.shape[axis]
    lower = (jnp.arange(size)[:, None] >= jnp.arange(size)[None, :]).astype(F32)
    moved = jnp.tensordot(lower, a.astype(F32), axes=(1, axis), precision=lax.Precision.HIGHEST)
    return jnp.moveaxis(moved, 0, axis)


def prefix(value, axis, combine, identity, reverse):
    peers, place = (lax.axis_size(axis), lax.axis_index(axis))
    everything = jax.tree.map(
        lambda part, kind: lax.all_gather(part.astype(kind), axis),
        value,
        jax.tree.map(lambda a: jnp.bfloat16 if a.dtype == jnp.float32 else a.dtype, value),
    )
    start = jax.tree.map(
        lambda part, zero: jnp.broadcast_to(jnp.asarray(zero, part.dtype), part.shape),
        value,
        identity,
    )

    def lap(k, before):
        at = peers - 1 - k if reverse else k
        reached = at > place if reverse else at < place
        new = combine(
            before, jax.tree.map(lambda part, own: part[at].astype(own.dtype), everything, value)
        )
        return jax.tree.map(lambda a, b: jnp.where(reached, a, b), new, before)

    return lax.fori_loop(0, peers, lap, start)


def local_pass(inputs, keys, queries, logs):
    rows, heads_local, width = inputs.shape
    blocks = rows // SPAN
    xblock = inputs.reshape(blocks, SPAN, heads_local, width)
    kblock_low = keys.reshape(blocks, SPAN, keys.shape[1])
    qblock_low = queries.reshape(blocks, SPAN, queries.shape[1])
    kblock = kblock_low.astype(jnp.float32)
    qblock = qblock_low.astype(jnp.float32)
    lcum = running(logs.reshape(blocks, SPAN, heads_local), 1)
    scores = jnp.einsum("cqn,csn->cqs", qblock_low, kblock_low, preferred_element_type=jnp.float32)
    causal = jnp.arange(SPAN)[:, None] >= jnp.arange(SPAN)[None, :]
    gap = lcum[:, :, None, :] - lcum[:, None, :, :]
    weight = jnp.where(
        causal[None, :, :, None], jnp.exp(jnp.where(causal[None, :, :, None], gap, 0.0)), 0.0
    )
    intra = jnp.einsum(
        "cqsh,cshp->cqhp", scores[..., None] * weight, xblock, precision=lax.Precision.HIGHEST
    )
    tail = jnp.exp(lcum[:, -1:, :] - lcum)
    block_state = jnp.einsum(
        "csn,cshp->chnp", kblock, xblock * tail[..., None], precision=lax.Precision.HIGHEST
    )
    block_log = lcum[:, -1, :]

    def advance(state, item):
        log_c, new_state = item
        return (jnp.exp(log_c)[:, None, None] * state + new_state, state)

    start = jnp.zeros((heads_local, keys.shape[1], width), jnp.float32)
    final, entering = lax.scan(advance, start, (block_log, block_state))
    total_log = jnp.sum(block_log, axis=0)
    return ((qblock, lcum, intra, entering, block_log), (total_log, final))


def finish(pieces, carried):
    qblock, lcum, intra, entering, block_log = pieces
    before = running(block_log, 0) - block_log
    enter_all = entering + jnp.exp(before)[:, :, None, None] * carried[None]
    inter = jnp.exp(lcum)[..., None] * jnp.einsum(
        "cqn,chnp->cqhp", qblock, enter_all, precision=lax.Precision.HIGHEST
    )
    total = intra + inter
    return total.reshape(-1, total.shape[2], total.shape[3])


def combine(earlier, later):
    return (earlier[0] + later[0], jnp.exp(later[0])[:, None, None] * earlier[1] + later[1])


def per_device(
    points, owner, local_order, codes, w_in, w_bc, decay_rate, dt_scale, skip_gain, w_out
):
    n_curve = lax.axis_size("curve")
    n_model = lax.axis_size("mp")
    count = points.shape[0]
    rows = 2 * count
    slots = rows // n_curve
    heads_local = HEADS // n_model
    model_index = lax.axis_index("mp")
    order = local_order[0]
    sorted_owner = owner[:, 0][order]
    onehot = (sorted_owner[:, None] == jnp.arange(n_curve, dtype=jnp.int32)[None, :]).astype(
        jnp.int32
    )
    slot = jnp.sum(running(onehot, 0) * onehot, axis=1).astype(jnp.int32) - 1
    target = jnp.zeros((count,), jnp.int32).at[order].set(sorted_owner * slots + slot)
    send_codes = jnp.zeros((rows,), jnp.int32).at[target].set(codes)
    send_rows = jnp.zeros((rows, points.shape[1]), points.dtype).at[target].set(points)
    arrived, arrived_codes = (
        lax.all_to_all(send_rows, "curve", split_axis=0, concat_axis=0, tiled=True),
        lax.all_to_all(send_codes, "curve", split_axis=0, concat_axis=0, tiled=True),
    )
    proj_sum = jnp.einsum("rk,kjc->rjc", arrived, w_in, preferred_element_type=jnp.float32)
    bc_sum = jnp.einsum("rk,kjc->rjc", arrived, w_bc, preferred_element_type=jnp.float32)
    proj = lax.optimization_barrier(proj_sum.astype(jnp.bfloat16)).astype(jnp.float32)
    bc = bc_sum.astype(jnp.bfloat16)
    code_f = arrived_codes.astype(jnp.float32)
    rates = lax.dynamic_slice_in_dim(decay_rate, model_index * heads_local, heads_local, 1)
    steps_dt = lax.dynamic_slice_in_dim(dt_scale, model_index * heads_local, heads_local, 1)
    skips = lax.dynamic_slice_in_dim(skip_gain, model_index * heads_local, heads_local, 1)
    pieces = []
    summaries = []
    xparts = []
    gates = []
    for direction in range(2):
        xh = proj[:, 2 * direction].reshape(rows, heads_local, HEADDIM)
        gates.append(proj[:, 2 * direction + 1].reshape(rows, heads_local, HEADDIM))
        xparts.append(xh)
        inputs = xh * steps_dt[direction][None, :, None]
        keys = bc[:, 2 * direction]
        queries = bc[:, 2 * direction + 1]
        logs = -rates[direction][None, :] * code_f[:, None]
        if direction == 1:
            inputs, keys, queries, logs = (
                jnp.flip(inputs, 0),
                jnp.flip(keys, 0),
                jnp.flip(queries, 0),
                jnp.flip(logs, 0),
            )
        kept, summary = local_pass(inputs, keys, queries, logs)
        pieces.append(kept)
        summaries.append(summary)
    ident = (jnp.zeros((heads_local,), jnp.float32), jnp.zeros_like(summaries[0][1]))
    forward_in = prefix(summaries[0], "curve", combine, ident, False)[1]
    backward_in = prefix(summaries[1], "curve", combine, ident, True)[1]
    carried_all = (forward_in, backward_in)
    normed = []
    for direction in range(2):
        outs = finish(pieces[direction], carried_all[direction])
        if direction == 1:
            outs = jnp.flip(outs, 0)
        outs = outs + skips[direction][None, :, None] * xparts[direction]
        value = outs * jax.nn.silu(gates[direction])
        value = value / jnp.sqrt(jnp.mean(value * value, axis=-1, keepdims=True) + 1e-05)
        normed.append(value.astype(jnp.bfloat16).reshape(rows, heads_local * HEADDIM))
    stacked = jnp.stack(normed, axis=1)
    w_rows = lax.dynamic_slice_in_dim(
        w_out, model_index * heads_local * HEADDIM, heads_local * HEADDIM, 1
    )
    terms = jnp.einsum("rdk,dkc->rc", stacked, w_rows, preferred_element_type=jnp.float32)
    summed = lax.psum_scatter(terms.astype(jnp.bfloat16), "mp", scatter_dimension=1, tiled=True)
    back = lax.all_to_all(summed, "curve", split_axis=0, concat_axis=0, tiled=True)
    return back[target]


def mm(a, b, ca=1, cb=0):
    return lax.dot_general(a, b, (((ca,), (cb,)), ((), ())), preferred_element_type=F32)


def iota(shape, dim):
    return lax.broadcasted_iota(jnp.int32, shape, dim)


def as_bf16(mask):
    return jnp.where(mask, 1.0, 0.0).astype(BF16)


def layer_kernel(
    nc,
    slots,
    pts,
    own,
    order,
    codes,
    w_in,
    w_bc,
    rate,
    dt,
    skip,
    w_out,
    out,
    w,
    wo,
    wsem,
    sendb,
    tt,
    csend,
    carr,
    arr,
    proj,
    cols,
    yin,
    ctot,
    cst,
    ent,
    pre,
    ssend,
    srecv,
    dsend,
    drecv,
    carried,
    part,
    recva,
    sendx,
    recvx,
    sumc,
    back,
    zs,
    zr,
    cs,
    cr,
    xs,
    xr,
    ps,
    pr,
    fs,
    fr,
    ss,
    sr,
    ds,
    dr,
    gs,
    gr,
    hs,
    hr,
    bs,
    br,
):
    count = pts.shape[0]
    share = slots // 4
    halves = slots // SPAN
    chunks = nc * halves
    me = lax.axis_index("curve")
    q = lax.axis_index("mp")
    core = lax.rem(q, 2)
    xx = lax.div(q, 2)
    other_core = q + 1 - 2 * core
    other_x = q + 2 - 4 * xx
    to_core = {"mp": other_core}
    to_x = {"mp": other_x}

    def after(k):
        return lax.rem(me + k, nc)

    def before(k):
        return lax.rem(me - k + nc, nc)

    def copy(src, dst, s, r, where):
        return pltpu.make_async_remote_copy(
            src_ref=src, dst_ref=dst, send_sem=s, recv_sem=r, device_id=where, device_id_type=MESH
        )

    def at(start, size):
        return pl.ds(pl.multiple_of(start, size), size)

    loads = [
        pltpu.make_async_copy(w_in, w.at[:, 0:1024], wsem.at[0]),
        pltpu.make_async_copy(w_out.at[:, at(q * 256, 256), :], wo, wsem.at[1]),
    ]
    for load in loads:
        load.start()

    def lane_values(table, d):
        head = iota((1, 256), 1) // HEADDIM
        made = jnp.full((1, 256), table[d, q * 4], F32)
        for h in range(1, 4):
            made = jnp.where(head == h, table[d, q * 4 + h], made)
        return made

    rate_lane = [lane_values(rate, d) * LOG2E for d in range(2)]
    dt_lane = [lane_values(dt, d) for d in range(2)]
    skip_lane = [lane_values(skip, d) for d in range(2)]

    barrier = pltpu.get_barrier_semaphore()
    for k in range(1, nc):
        pl.semaphore_signal(barrier, inc=1, device_id={"curve": after(k)}, device_id_type=MESH)
    for there in (to_core, to_x):
        pl.semaphore_signal(barrier, inc=1, device_id=there, device_id_type=MESH)

    picks = as_bf16(iota((count, count), 0) == order[...])
    own8 = jnp.broadcast_to(own[...].astype(F32), (8, count)).astype(BF16)
    sorted8 = mm(own8, picks)
    hot8 = as_bf16(sorted8 == iota((8, count), 0).astype(F32))
    upper = as_bf16(iota((count, count), 0) <= iota((count, count), 1))
    counts = mm(hot8, upper)
    slot = jnp.sum(counts * hot8.astype(F32), axis=0, keepdims=True) - 1.0
    target = sorted8[0:1] * float(slots) + slot
    high = jnp.floor(target * (1.0 / 64.0))
    low = target - high * 64.0
    split8 = jnp.where(iota((8, count), 0) == 0, high, low).astype(BF16)
    trow8 = mm(split8, picks, 1, 1)
    trow = trow8[0:1] * 64.0 + trow8[1:2]
    tcol8 = mm(picks, split8, 1, 1)
    tcol = tcol8[:, 0:1] * 64.0 + tcol8[:, 1:2]

    def routed(t):
        place = (iota((share, count), 0) + (t * slots + q * share)).astype(F32)
        return mm(as_bf16(place == trow), pts[...]).astype(BF16)

    def zcopy(k):
        return copy(
            sendb.at[k],
            arr.at[at(me * slots + q * share, share)],
            zs.at[k],
            zr.at[k],
            {"curve": after(k)},
        )

    def ccopy(k):
        return copy(csend.at[after(k)], carr.at[me], cs.at[k], cr.at[k], {"curve": after(k)})

    def mine(s, who):
        return arr.at[at(s * slots + who * share, share)]

    def xcopy(k):
        s = before(k)
        return copy(mine(s, q), mine(s, q), xs.at[k], xr.at[k], to_x)

    def pcopy(k):
        s = before(k)
        return copy(mine(s, q), mine(s, q), ps.at[k], pr.at[k], to_core)

    def fcopy(k):
        s = before(k)
        return copy(mine(s, other_x), mine(s, other_x), fs.at[k], fr.at[k], to_core)

    first = routed(after(nc - 1))
    sendb[nc - 1] = first
    pl.semaphore_wait(barrier, nc + 1)
    zcopy(nc - 1).start()
    for k in range(nc - 2, 0, -1):
        sendb[k] = routed(after(k))
        zcopy(k).start()
    arr[at(me * slots + q * share, share)] = routed(me)
    xcopy(0).start()
    pcopy(0).start()

    codef = codes[...].astype(F32)
    chigh = jnp.floor(codef * (1.0 / 128.0))
    code8 = jnp.where(iota((8, count), 0) == 0, chigh, codef - chigh * 128.0).astype(BF16)
    for t in range(nc):
        hot = as_bf16(tcol == (iota((count, slots), 1) + t * slots).astype(F32))
        tt[t] = hot
        made = mm(code8, hot)
        for h in range(halves):
            csend[t, h] = made[:, h * SPAN : (h + 1) * SPAN]
    for k in range(1, nc):
        ccopy(k).start()
    carr[me] = csend[me]

    for j in range(4):
        w[:, 1024 + 128 * j : 1152 + 128 * j] = jnp.concatenate(
            [w_bc[:, 64 * j : 64 * j + 64], jnp.zeros((w_bc.shape[0], 64), BF16)], axis=1
        )
    for load in loads:
        load.wait()

    above = iota((SPAN, SPAN), 0) <= iota((SPAN, SPAN), 1)
    below = iota((SPAN, SPAN), 0) >= iota((SPAN, SPAN), 1)

    def project(s):
        def half(h, _):
            c = s * halves + h
            rows = at(c * SPAN, SPAN)
            made = mm(arr[rows, :], w[...]).astype(BF16)
            proj[rows, :] = made
            c8 = carr[s, h].astype(BF16)
            run8 = mm(c8, as_bf16(above))
            srow = run8[0:1] * 128.0 + run8[1:2]
            own_row = carr[s, h]
            erow = srow - (own_row[0:1] * 128.0 + own_row[1:2])
            scol8 = mm(as_bf16(below), c8, 1, 1)
            scol = scol8[:, 0:1] * 128.0 + scol8[:, 1:2]
            strict = as_bf16(iota((SPAN, SPAN), 0) > iota((SPAN, SPAN), 1))
            ecol8 = mm(strict, c8, 1, 1)
            ecol = ecol8[:, 0:1] * 128.0 + ecol8[:, 1:2]
            cols[0, rows, :] = jnp.broadcast_to(scol, (SPAN, 128))
            cols[1, rows, :] = jnp.broadcast_to(ecol, (SPAN, 128))
            total = srow[:, SPAN - 1 : SPAN]
            ctot[c] = jnp.broadcast_to(total, (8, 256))
            for d, reach in ((0, scol - total), (1, -ecol)):
                tail = jnp.exp2(rate_lane[d] * reach)
                xt = (made[:, 512 * d : 512 * d + 256].astype(F32) * tail).astype(BF16)
                keys = made[:, 1024 + 256 * d : 1152 + 256 * d]
                cst[d, c] = mm(keys, xt, 0, 0)[0:64]
            for d in range(2):
                x = made[:, 512 * d : 512 * d + 256]
                keys = made[:, 1024 + 256 * d : 1152 + 256 * d]
                queries = made[:, 1152 + 256 * d : 1280 + 256 * d]
                scores = jnp.where(below if d == 0 else above, mm(queries, keys, 1, 1), 0.0)
                gap = jnp.minimum((srow - scol) if d == 0 else (ecol - erow), 0.0)
                left = iota((SPAN, 128), 1) < 64
                for p in range(2):
                    xp = x[:, 128 * p : 128 * p + 128]
                    nothing = jnp.zeros_like(xp)
                    weights = [
                        (scores * jnp.exp2((rate[d, q * 4 + 2 * p + g] * LOG2E) * gap)).astype(BF16)
                        for g in range(2)
                    ]
                    yin[d, rows, 128 * p : 128 * p + 128] = mm(
                        jnp.concatenate(weights, axis=1),
                        jnp.concatenate(
                            [jnp.where(left, xp, nothing), jnp.where(left, nothing, xp)], axis=0
                        ),
                    )
            return 0

        lax.fori_loop(0, halves, half, 0)

    def complete(k):
        pcopy(k).wait_recv()
        fcopy(k).wait_recv()
        if k:
            ccopy(k).wait_recv()
        project(before(k))

    xcopy(0).wait_recv()
    fcopy(0).start()
    last = 0
    for k in range(nc - 1, 0, -1):
        zcopy(k).wait_recv()
        xcopy(k).start()
        pcopy(k).start()
        complete(last)
        xcopy(k).wait_recv()
        fcopy(k).start()
        last = k
    complete(last)

    for d in range(2):
        state = jnp.zeros((64, 256), F32)
        passed = jnp.zeros((8, 256), F32)
        for step in range(chunks):
            c = step if d == 0 else chunks - 1 - step
            ent[d, c] = state
            pre[d, c] = passed
            gone = ctot[c]
            state = jnp.exp2(-rate_lane[d] * gone[0:1]) * state + cst[d, c]
            passed = passed + gone
        ssend[d] = state.astype(BF16)
        dsend[...] = passed

    def scopy(k):
        t = after(k)
        which = jnp.where(t > me, 0, 1)
        return copy(ssend.at[which], srecv.at[k], ss.at[k], sr.at[k], {"curve": t})

    def dcopy(k):
        return copy(dsend, drecv.at[k], ds.at[k], dr.at[k], {"curve": after(k)})

    for k in range(1, nc):
        scopy(k).start()
        dcopy(k).start()
    for k in range(1, nc):
        scopy(k).wait_recv()
        dcopy(k).wait_recv()
    for d in range(2):
        total = jnp.zeros((64, 256), F32)
        for k in range(1, nc):
            s = before(k)
            gap = jnp.zeros((1, 256), F32)
            for j in range(1, nc):
                u = before(j)
                if d == 0:
                    inside = jnp.logical_and(u > s, u < me)
                else:
                    inside = jnp.logical_and(u < s, u > me)
                gap = gap + jnp.where(inside, drecv[j][0:1], 0.0)
            counted = (s < me) if d == 0 else (s > me)
            term = jnp.exp2(-rate_lane[d] * gap) * srecv[k].astype(F32)
            total = total + jnp.where(counted, term, 0.0)
        carried[d] = total

    def attend(c):
        rows = at(c * SPAN, SPAN)
        normed = []
        for d in range(2):
            x = proj[rows, 512 * d : 512 * d + 256]
            z = proj[rows, 512 * d + 256 : 512 * d + 512].astype(F32)
            queries = proj[rows, 1152 + 256 * d : 1280 + 256 * d]
            col = cols[d, rows, :]
            col = jnp.concatenate([col, col], axis=1)
            lanes = rate_lane[d]
            entering = ent[d, c] + jnp.exp2(-lanes * pre[d, c][0:1]) * carried[d]
            reach = -col if d == 0 else col - ctot[c][0:1]
            inter = mm(queries[:, 0:64], entering.astype(BF16)) * jnp.exp2(lanes * reach)
            y = dt_lane[d] * (yin[d, rows, :] + inter) + skip_lane[d] * x.astype(F32)
            v = y * (z / (1.0 + jnp.exp(-z)))
            same = as_bf16((iota((256, 256), 0) // 64) == (iota((256, 256), 1) // 64))
            mean = mm((v * v).astype(BF16), same) * (1.0 / 64.0)
            normed.append((v * lax.rsqrt(mean + 1e-05)).astype(BF16))
        terms = (mm(normed[0], wo[0]) + mm(normed[1], wo[1])).astype(BF16)
        for m in range(4):
            part[m % 2, m // 2, rows, :] = terms[:, 128 * m : 128 * m + 128]

    turns = list(range(nc - 1, -1, -1))

    def turn(j):
        return turns[j // halves]

    def rows_of(j):
        return at((after(turn(j)) * halves + j % halves) * SPAN, SPAN)

    def acopy(j):
        rows = rows_of(j)
        return copy(part.at[1 - core, :, rows], recva.at[:, rows], gs.at[j], gr.at[j], to_core)

    def bcopy(j):
        rows = rows_of(j)
        return copy(sendx.at[rows], recvx.at[rows], hs.at[j], hr.at[j], to_x)

    def backcopy(j):
        landing = at((me * halves + j % halves) * SPAN, SPAN)
        return copy(
            sumc.at[rows_of(j)], back.at[landing], bs.at[j], br.at[j], {"curve": after(turn(j))}
        )

    def cross(j):
        acopy(j).wait_recv()
        rows = rows_of(j)
        sendx[rows, :] = (
            part[core, 1 - xx, rows, :].astype(F32) + recva[1 - xx, rows, :].astype(F32)
        ).astype(BF16)
        bcopy(j).start()

    def home(j):
        bcopy(j).wait_recv()
        rows = rows_of(j)
        total = (
            part[core, xx, rows, :].astype(F32)
            + recva[xx, rows, :].astype(F32)
            + recvx[rows, :].astype(F32)
        ).astype(BF16)
        if turn(j):
            sumc[rows, :] = total
            backcopy(j).start()
        else:
            back[rows, :] = total

    for step in range(chunks + 3):
        if step < chunks:
            attend(after(turn(step)) * halves + step % halves)
            acopy(step).start()
        if 1 <= step <= chunks:
            cross(step - 1)
        if 3 <= step:
            home(step - 3)
    for j in range(chunks - halves):
        backcopy(j).wait_recv()
    total = jnp.zeros((count, 128), F32)
    for t in range(nc):
        total = total + mm(tt[t], back[t * slots : (t + 1) * slots, :])
    out[...] = total.astype(BF16)

    for k in range(nc):
        xcopy(k).wait_send()
        pcopy(k).wait_send()
        fcopy(k).wait_send()
        if k:
            zcopy(k).wait_send()
            ccopy(k).wait_send()
            scopy(k).wait_send()
            dcopy(k).wait_send()
    for j in range(chunks):
        acopy(j).wait_send()
        bcopy(j).wait_send()
        if turn(j):
            backcopy(j).wait_send()


def fused_device(
    points, owner, local_order, codes, w_in, w_bc, decay_rate, dt_scale, skip_gain, w_out
):
    nc = lax.axis_size("curve")
    n_model = lax.axis_size("mp")
    count, width = points.shape
    rows = 2 * count
    slots = rows // nc
    halves = slots // SPAN
    chunks = nc * halves
    cut = HEADS // n_model * HEADDIM
    vm = pltpu.VMEM
    sem = pltpu.SemaphoreType.DMA
    vspec = pl.BlockSpec(memory_space=pltpu.VMEM)
    hbm = pl.BlockSpec(memory_space=pl.ANY)
    sspec = pl.BlockSpec(memory_space=pltpu.SMEM)
    return pl.pallas_call(
        functools.partial(layer_kernel, nc, slots),
        out_shape=jax.ShapeDtypeStruct((count, width // 4), BF16),
        in_specs=[vspec] * 4 + [hbm, vspec] + [sspec] * 3 + [hbm],
        out_specs=vspec,
        scratch_shapes=[
            vm((width, 6 * cut), BF16),
            vm((2, cut, width), BF16),
            sem((2,)),
            vm((nc, slots // 4, width), BF16),
            vm((nc, count, slots), BF16),
            vm((nc, halves, 8, SPAN), F32),
            vm((nc, halves, 8, SPAN), F32),
            vm((rows, width), BF16),
            vm((rows, 6 * cut), BF16),
            vm((2, rows, 128), F32),
            vm((2, rows, 256), F32),
            vm((chunks, 8, 256), F32),
            vm((2, chunks, 64, 256), F32),
            vm((2, chunks, 64, 256), F32),
            vm((2, chunks, 8, 256), F32),
            vm((2, 64, 256), BF16),
            vm((nc, 64, 256), BF16),
            vm((8, 256), F32),
            vm((nc, 8, 256), F32),
            vm((2, 64, 256), F32),
            vm((2, 2, rows, 128), BF16),
            vm((2, rows, 128), BF16),
            vm((rows, 128), BF16),
            vm((rows, 128), BF16),
            vm((rows, 128), BF16),
            vm((rows, 128), BF16),
        ]
        + [sem((nc,))] * 14
        + [sem((chunks,))] * 6,
        compiler_params=pltpu.CompilerParams(
            collective_id=0, has_side_effects=True, vmem_limit_bytes=56 * 1024 * 1024
        ),
    )(
        points,
        owner.reshape(1, count),
        local_order,
        codes.reshape(1, count),
        w_in.reshape(width, 4 * cut),
        w_bc.reshape(width, 256),
        decay_rate,
        dt_scale,
        skip_gain,
        w_out,
    )


def solution(mesh):
    placed = (
        P(("groups", "curve"), None),
        P(("groups", "curve"), None),
        P(("groups", "curve"), None),
        P(("groups", "curve")),
        P(None, None, "mp"),
        P(),
        P(),
        P(),
        P(),
        P(),
    )
    sizes = dict(mesh.shape)

    def body(points, *rest):
        slots = 2 * points.shape[0] // sizes["curve"]
        if sizes["mp"] == 4 and slots % SPAN == 0 and sizes["curve"] <= 8:
            return fused_device(points, *rest)
        return per_device(points, *rest)

    return jax.shard_map(
        body,
        mesh=mesh,
        in_specs=placed,
        out_specs=P(("groups", "curve"), "mp"),
        check_vma=False,
    )
```

```python
import functools

import jax
import jax.numpy as jnp
from jax import lax
from jax.experimental import pallas as pl
from jax.experimental.pallas import tpu as pltpu
from jax.sharding import PartitionSpec as P

HEADS = 16
HEADDIM = 64
SPAN = 256
LOG2E = 1.4426950408889634
F32 = jnp.float32
BF16 = jnp.bfloat16
MESH = pl.DeviceIdType.MESH


def running(a, axis):
    size = a.shape[axis]
    lower = (jnp.arange(size)[:, None] >= jnp.arange(size)[None, :]).astype(F32)
    moved = jnp.tensordot(lower, a.astype(F32), axes=(1, axis), precision=lax.Precision.HIGHEST)
    return jnp.moveaxis(moved, 0, axis)


def prefix(value, axis, combine, identity, reverse):
    peers, place = (lax.axis_size(axis), lax.axis_index(axis))
    everything = jax.tree.map(
        lambda part, kind: lax.all_gather(part.astype(kind), axis),
        value,
        jax.tree.map(lambda a: jnp.bfloat16 if a.dtype == jnp.float32 else a.dtype, value),
    )
    start = jax.tree.map(
        lambda part, zero: jnp.broadcast_to(jnp.asarray(zero, part.dtype), part.shape),
        value,
        identity,
    )

    def lap(k, before):
        at = peers - 1 - k if reverse else k
        reached = at > place if reverse else at < place
        new = combine(
            before, jax.tree.map(lambda part, own: part[at].astype(own.dtype), everything, value)
        )
        return jax.tree.map(lambda a, b: jnp.where(reached, a, b), new, before)

    return lax.fori_loop(0, peers, lap, start)


def local_pass(inputs, keys, queries, logs):
    rows, heads_local, width = inputs.shape
    blocks = rows // SPAN
    xblock = inputs.reshape(blocks, SPAN, heads_local, width)
    kblock_low = keys.reshape(blocks, SPAN, keys.shape[1])
    qblock_low = queries.reshape(blocks, SPAN, queries.shape[1])
    kblock = kblock_low.astype(jnp.float32)
    qblock = qblock_low.astype(jnp.float32)
    lcum = running(logs.reshape(blocks, SPAN, heads_local), 1)
    scores = jnp.einsum("cqn,csn->cqs", qblock_low, kblock_low, preferred_element_type=jnp.float32)
    causal = jnp.arange(SPAN)[:, None] >= jnp.arange(SPAN)[None, :]
    gap = lcum[:, :, None, :] - lcum[:, None, :, :]
    weight = jnp.where(
        causal[None, :, :, None], jnp.exp(jnp.where(causal[None, :, :, None], gap, 0.0)), 0.0
    )
    intra = jnp.einsum(
        "cqsh,cshp->cqhp", scores[..., None] * weight, xblock, precision=lax.Precision.HIGHEST
    )
    tail = jnp.exp(lcum[:, -1:, :] - lcum)
    block_state = jnp.einsum(
        "csn,cshp->chnp", kblock, xblock * tail[..., None], precision=lax.Precision.HIGHEST
    )
    block_log = lcum[:, -1, :]

    def advance(state, item):
        log_c, new_state = item
        return (jnp.exp(log_c)[:, None, None] * state + new_state, state)

    start = jnp.zeros((heads_local, keys.shape[1], width), jnp.float32)
    final, entering = lax.scan(advance, start, (block_log, block_state))
    total_log = jnp.sum(block_log, axis=0)
    return ((qblock, lcum, intra, entering, block_log), (total_log, final))


def finish(pieces, carried):
    qblock, lcum, intra, entering, block_log = pieces
    before = running(block_log, 0) - block_log
    enter_all = entering + jnp.exp(before)[:, :, None, None] * carried[None]
    inter = jnp.exp(lcum)[..., None] * jnp.einsum(
        "cqn,chnp->cqhp", qblock, enter_all, precision=lax.Precision.HIGHEST
    )
    total = intra + inter
    return total.reshape(-1, total.shape[2], total.shape[3])


def combine(earlier, later):
    return (earlier[0] + later[0], jnp.exp(later[0])[:, None, None] * earlier[1] + later[1])


def per_device(
    points, owner, local_order, codes, w_in, w_bc, decay_rate, dt_scale, skip_gain, w_out
):
    n_curve = lax.axis_size("curve")
    n_model = lax.axis_size("mp")
    count = points.shape[0]
    rows = 2 * count
    slots = rows // n_curve
    heads_local = HEADS // n_model
    model_index = lax.axis_index("mp")
    order = local_order[0]
    sorted_owner = owner[:, 0][order]
    onehot = (sorted_owner[:, None] == jnp.arange(n_curve, dtype=jnp.int32)[None, :]).astype(
        jnp.int32
    )
    slot = jnp.sum(running(onehot, 0) * onehot, axis=1).astype(jnp.int32) - 1
    target = jnp.zeros((count,), jnp.int32).at[order].set(sorted_owner * slots + slot)
    send_codes = jnp.zeros((rows,), jnp.int32).at[target].set(codes)
    send_rows = jnp.zeros((rows, points.shape[1]), points.dtype).at[target].set(points)
    arrived, arrived_codes = (
        lax.all_to_all(send_rows, "curve", split_axis=0, concat_axis=0, tiled=True),
        lax.all_to_all(send_codes, "curve", split_axis=0, concat_axis=0, tiled=True),
    )
    proj_sum = jnp.einsum("rk,kjc->rjc", arrived, w_in, preferred_element_type=jnp.float32)
    bc_sum = jnp.einsum("rk,kjc->rjc", arrived, w_bc, preferred_element_type=jnp.float32)
    proj = lax.optimization_barrier(proj_sum.astype(jnp.bfloat16)).astype(jnp.float32)
    bc = bc_sum.astype(jnp.bfloat16)
    code_f = arrived_codes.astype(jnp.float32)
    rates = lax.dynamic_slice_in_dim(decay_rate, model_index * heads_local, heads_local, 1)
    steps_dt = lax.dynamic_slice_in_dim(dt_scale, model_index * heads_local, heads_local, 1)
    skips = lax.dynamic_slice_in_dim(skip_gain, model_index * heads_local, heads_local, 1)
    pieces = []
    summaries = []
    xparts = []
    gates = []
    for direction in range(2):
        xh = proj[:, 2 * direction].reshape(rows, heads_local, HEADDIM)
        gates.append(proj[:, 2 * direction + 1].reshape(rows, heads_local, HEADDIM))
        xparts.append(xh)
        inputs = xh * steps_dt[direction][None, :, None]
        keys = bc[:, 2 * direction]
        queries = bc[:, 2 * direction + 1]
        logs = -rates[direction][None, :] * code_f[:, None]
        if direction == 1:
            inputs, keys, queries, logs = (
                jnp.flip(inputs, 0),
                jnp.flip(keys, 0),
                jnp.flip(queries, 0),
                jnp.flip(logs, 0),
            )
        kept, summary = local_pass(inputs, keys, queries, logs)
        pieces.append(kept)
        summaries.append(summary)
    ident = (jnp.zeros((heads_local,), jnp.float32), jnp.zeros_like(summaries[0][1]))
    forward_in = prefix(summaries[0], "curve", combine, ident, False)[1]
    backward_in = prefix(summaries[1], "curve", combine, ident, True)[1]
    carried_all = (forward_in, backward_in)
    normed = []
    for direction in range(2):
        outs = finish(pieces[direction], carried_all[direction])
        if direction == 1:
            outs = jnp.flip(outs, 0)
        outs = outs + skips[direction][None, :, None] * xparts[direction]
        value = outs * jax.nn.silu(gates[direction])
        value = value / jnp.sqrt(jnp.mean(value * value, axis=-1, keepdims=True) + 1e-05)
        normed.append(value.astype(jnp.bfloat16).reshape(rows, heads_local * HEADDIM))
    stacked = jnp.stack(normed, axis=1)
    w_rows = lax.dynamic_slice_in_dim(
        w_out, model_index * heads_local * HEADDIM, heads_local * HEADDIM, 1
    )
    terms = jnp.einsum("rdk,dkc->rc", stacked, w_rows, preferred_element_type=jnp.float32)
    summed = lax.psum_scatter(terms.astype(jnp.bfloat16), "mp", scatter_dimension=1, tiled=True)
    back = lax.all_to_all(summed, "curve", split_axis=0, concat_axis=0, tiled=True)
    return back[target]


def mm(a, b, ca=1, cb=0):
    return lax.dot_general(a, b, (((ca,), (cb,)), ((), ())), preferred_element_type=F32)


def iota(shape, dim):
    return lax.broadcasted_iota(jnp.int32, shape, dim)


def as_bf16(mask):
    return jnp.where(mask, 1.0, 0.0).astype(BF16)


def layer_kernel(
    nc,
    slots,
    pts,
    own,
    order,
    codes,
    w_in,
    w_bc,
    rate,
    dt,
    skip,
    w_out,
    out,
    w,
    wo,
    wsem,
    sendb,
    tt,
    csend,
    carr,
    arr,
    proj,
    cols,
    yin,
    ctot,
    cst,
    ent,
    pre,
    ssend,
    srecv,
    dsend,
    drecv,
    carried,
    part,
    recva,
    sendx,
    recvx,
    sumc,
    back,
    zs,
    zr,
    cs,
    cr,
    xs,
    xr,
    ps,
    pr,
    fs,
    fr,
    ss,
    sr,
    ds,
    dr,
    gs,
    gr,
    hs,
    hr,
    bs,
    br,
):
    count = pts.shape[0]
    share = slots // 4
    halves = slots // SPAN
    chunks = nc * halves
    me = lax.axis_index("curve")
    q = lax.axis_index("mp")
    core = lax.rem(q, 2)
    xx = lax.div(q, 2)
    other_core = q + 1 - 2 * core
    other_x = q + 2 - 4 * xx
    to_core = {"mp": other_core}
    to_x = {"mp": other_x}

    def after(k):
        return lax.rem(me + k, nc)

    def before(k):
        return lax.rem(me - k + nc, nc)

    def copy(src, dst, s, r, where):
        return pltpu.make_async_remote_copy(
            src_ref=src, dst_ref=dst, send_sem=s, recv_sem=r, device_id=where, device_id_type=MESH
        )

    def at(start, size):
        return pl.ds(pl.multiple_of(start, size), size)

    loads = [
        pltpu.make_async_copy(w_in, w.at[:, 0:1024], wsem.at[0]),
        pltpu.make_async_copy(w_out.at[:, at(q * 256, 256), :], wo, wsem.at[1]),
    ]
    for load in loads:
        load.start()

    def lane_values(table, d):
        head = iota((1, 256), 1) // HEADDIM
        made = jnp.full((1, 256), table[d, q * 4], F32)
        for h in range(1, 4):
            made = jnp.where(head == h, table[d, q * 4 + h], made)
        return made

    rate_lane = [lane_values(rate, d) * LOG2E for d in range(2)]
    dt_lane = [lane_values(dt, d) for d in range(2)]
    skip_lane = [lane_values(skip, d) for d in range(2)]

    barrier = pltpu.get_barrier_semaphore()
    for k in range(1, nc):
        pl.semaphore_signal(barrier, inc=1, device_id={"curve": after(k)}, device_id_type=MESH)
    for there in (to_core, to_x):
        pl.semaphore_signal(barrier, inc=1, device_id=there, device_id_type=MESH)

    picks = as_bf16(iota((count, count), 0) == order[...])
    own8 = jnp.broadcast_to(own[...].astype(F32), (8, count)).astype(BF16)
    sorted8 = mm(own8, picks)
    hot8 = as_bf16(sorted8 == iota((8, count), 0).astype(F32))
    upper = as_bf16(iota((128, 128), 0) <= iota((128, 128), 1))
    stripes = range(count // 128)
    runs = mm(jnp.concatenate([hot8[:, 128 * b : 128 * b + 128] for b in stripes], axis=0), upper)
    base = jnp.zeros((8, 1), F32)
    pieces = []
    for b in stripes:
        run = runs[8 * b : 8 * b + 8]
        pieces.append(run + base)
        base = base + run[:, 127:128]
    counts = jnp.concatenate(pieces, axis=1)
    slot = jnp.sum(counts * hot8.astype(F32), axis=0, keepdims=True) - 1.0
    target = sorted8[0:1] * float(slots) + slot
    high = jnp.floor(target * (1.0 / 64.0))
    low = target - high * 64.0
    split8 = jnp.where(iota((8, count), 0) == 0, high, low).astype(BF16)
    trow8 = mm(split8, picks, 1, 1)
    trow = trow8[0:1] * 64.0 + trow8[1:2]

    def routed(t):
        place = (iota((share, count), 0) + (t * slots + q * share)).astype(F32)
        return mm(as_bf16(place == trow), pts[...]).astype(BF16)

    def zcopy(k):
        return copy(
            sendb.at[k],
            arr.at[at(me * slots + q * share, share)],
            zs.at[k],
            zr.at[k],
            {"curve": after(k)},
        )

    def ccopy(k):
        return copy(csend.at[after(k)], carr.at[me], cs.at[k], cr.at[k], {"curve": after(k)})

    def mine(s, who):
        return arr.at[at(s * slots + who * share, share)]

    def xcopy(k):
        s = before(k)
        return copy(mine(s, q), mine(s, q), xs.at[k], xr.at[k], to_x)

    def pcopy(k):
        s = before(k)
        return copy(mine(s, q), mine(s, q), ps.at[k], pr.at[k], to_core)

    def fcopy(k):
        s = before(k)
        return copy(mine(s, other_x), mine(s, other_x), fs.at[k], fr.at[k], to_core)

    first = routed(after(nc - 1))
    sendb[nc - 1] = first
    pl.semaphore_wait(barrier, nc + 1)
    zcopy(nc - 1).start()
    for k in range(nc - 2, 0, -1):
        sendb[k] = routed(after(k))
        zcopy(k).start()
    arr[at(me * slots + q * share, share)] = routed(me)
    xcopy(0).start()
    pcopy(0).start()

    tcol8 = mm(picks, split8, 1, 1)
    tcol = tcol8[:, 0:1] * 64.0 + tcol8[:, 1:2]
    codef = codes[...].astype(F32)
    chigh = jnp.floor(codef * (1.0 / 128.0))
    code8 = jnp.where(iota((8, count), 0) == 0, chigh, codef - chigh * 128.0).astype(BF16)
    for t in range(nc):
        hot = as_bf16(tcol == (iota((count, slots), 1) + t * slots).astype(F32))
        tt[t] = hot
        made = mm(code8, hot)
        for h in range(halves):
            csend[t, h] = made[:, h * SPAN : (h + 1) * SPAN]
    for k in range(1, nc):
        ccopy(k).start()
    carr[me] = csend[me]

    for j in range(4):
        w[:, 1024 + 128 * j : 1152 + 128 * j] = jnp.concatenate(
            [w_bc[:, 64 * j : 64 * j + 64], jnp.zeros((w_bc.shape[0], 64), BF16)], axis=1
        )
    for load in loads:
        load.wait()

    above = iota((SPAN, SPAN), 0) <= iota((SPAN, SPAN), 1)
    below = iota((SPAN, SPAN), 0) >= iota((SPAN, SPAN), 1)

    def project(s):
        def half(h, _):
            c = s * halves + h
            rows = at(c * SPAN, SPAN)
            made = mm(arr[rows, :], w[...]).astype(BF16)
            proj[rows, :] = made
            c8 = carr[s, h].astype(BF16)
            run8 = mm(c8, as_bf16(above))
            srow = run8[0:1] * 128.0 + run8[1:2]
            own_row = carr[s, h]
            erow = srow - (own_row[0:1] * 128.0 + own_row[1:2])
            scol8 = mm(as_bf16(below), c8, 1, 1)
            scol = scol8[:, 0:1] * 128.0 + scol8[:, 1:2]
            strict = as_bf16(iota((SPAN, SPAN), 0) > iota((SPAN, SPAN), 1))
            ecol8 = mm(strict, c8, 1, 1)
            ecol = ecol8[:, 0:1] * 128.0 + ecol8[:, 1:2]
            cols[0, rows, :] = jnp.broadcast_to(scol, (SPAN, 128))
            cols[1, rows, :] = jnp.broadcast_to(ecol, (SPAN, 128))
            total = srow[:, SPAN - 1 : SPAN]
            ctot[c] = jnp.broadcast_to(total, (8, 256))
            for d, reach in ((0, scol - total), (1, -ecol)):
                tail = jnp.exp2(rate_lane[d] * reach)
                xt = (made[:, 512 * d : 512 * d + 256].astype(F32) * tail).astype(BF16)
                keys = made[:, 1024 + 256 * d : 1152 + 256 * d]
                cst[d, c] = mm(keys, xt, 0, 0)[0:64]
            for d in range(2):
                x = made[:, 512 * d : 512 * d + 256]
                keys = made[:, 1024 + 256 * d : 1152 + 256 * d]
                queries = made[:, 1152 + 256 * d : 1280 + 256 * d]
                scores = jnp.where(below if d == 0 else above, mm(queries, keys, 1, 1), 0.0)
                gap = jnp.minimum((srow - scol) if d == 0 else (ecol - erow), 0.0)
                left = iota((SPAN, 128), 1) < 64
                for p in range(2):
                    xp = x[:, 128 * p : 128 * p + 128]
                    nothing = jnp.zeros_like(xp)
                    lower_x = jnp.where(left, xp, nothing)
                    upper_x = jnp.where(left, nothing, xp)
                    for r in range(2):
                        lo, hi = (0, 128 * r + 128) if d == 0 else (128 * r, 256)
                        top = slice(128 * r, 128 * r + 128)
                        weights = [
                            (
                                scores[top, lo:hi]
                                * jnp.exp2((rate[d, q * 4 + 2 * p + g] * LOG2E) * gap[top, lo:hi])
                            ).astype(BF16)
                            for g in range(2)
                        ]
                        yin[d, at(c * SPAN + 128 * r, 128), 128 * p : 128 * p + 128] = mm(
                            jnp.concatenate(weights, axis=1),
                            jnp.concatenate([lower_x[lo:hi], upper_x[lo:hi]], axis=0),
                        )
            return 0

        lax.fori_loop(0, halves, half, 0)

    def complete(k):
        pcopy(k).wait_recv()
        fcopy(k).wait_recv()
        if k:
            ccopy(k).wait_recv()
        project(before(k))

    xcopy(0).wait_recv()
    fcopy(0).start()
    last = 0
    for k in range(nc - 1, 0, -1):
        zcopy(k).wait_recv()
        xcopy(k).start()
        pcopy(k).start()
        complete(last)
        xcopy(k).wait_recv()
        fcopy(k).start()
        last = k
    complete(last)

    for d in range(2):
        state = jnp.zeros((64, 256), F32)
        passed = jnp.zeros((8, 256), F32)
        for step in range(chunks):
            c = step if d == 0 else chunks - 1 - step
            ent[d, c] = state
            pre[d, c] = passed
            gone = ctot[c]
            state = jnp.exp2(-rate_lane[d] * gone[0:1]) * state + cst[d, c]
            passed = passed + gone
        ssend[d] = state.astype(BF16)
        dsend[...] = passed

    def scopy(k):
        t = after(k)
        which = jnp.where(t > me, 0, 1)
        return copy(ssend.at[which], srecv.at[k], ss.at[k], sr.at[k], {"curve": t})

    def dcopy(k):
        return copy(dsend, drecv.at[k], ds.at[k], dr.at[k], {"curve": after(k)})

    for k in range(1, nc):
        scopy(k).start()
        dcopy(k).start()
    for k in range(1, nc):
        scopy(k).wait_recv()
        dcopy(k).wait_recv()
    for d in range(2):
        total = jnp.zeros((64, 256), F32)
        for k in range(1, nc):
            s = before(k)
            gap = jnp.zeros((1, 256), F32)
            for j in range(1, nc):
                u = before(j)
                if d == 0:
                    inside = jnp.logical_and(u > s, u < me)
                else:
                    inside = jnp.logical_and(u < s, u > me)
                gap = gap + jnp.where(inside, drecv[j][0:1], 0.0)
            counted = (s < me) if d == 0 else (s > me)
            term = jnp.exp2(-rate_lane[d] * gap) * srecv[k].astype(F32)
            total = total + jnp.where(counted, term, 0.0)
        carried[d] = total

    def attend(c):
        rows = at(c * SPAN, SPAN)
        normed = []
        for d in range(2):
            x = proj[rows, 512 * d : 512 * d + 256]
            z = proj[rows, 512 * d + 256 : 512 * d + 512].astype(F32)
            queries = proj[rows, 1152 + 256 * d : 1280 + 256 * d]
            col = cols[d, rows, :]
            col = jnp.concatenate([col, col], axis=1)
            lanes = rate_lane[d]
            entering = ent[d, c] + jnp.exp2(-lanes * pre[d, c][0:1]) * carried[d]
            reach = -col if d == 0 else col - ctot[c][0:1]
            inter = mm(queries[:, 0:64], entering.astype(BF16)) * jnp.exp2(lanes * reach)
            y = dt_lane[d] * (yin[d, rows, :] + inter) + skip_lane[d] * x.astype(F32)
            v = y * (z / (1.0 + jnp.exp(-z)))
            same = as_bf16((iota((256, 256), 0) // 64) == (iota((256, 256), 1) // 64))
            mean = mm((v * v).astype(BF16), same) * (1.0 / 64.0)
            normed.append((v * lax.rsqrt(mean + 1e-05)).astype(BF16))
        terms = (mm(normed[0], wo[0]) + mm(normed[1], wo[1])).astype(BF16)
        for m in range(4):
            part[m % 2, m // 2, rows, :] = terms[:, 128 * m : 128 * m + 128]

    turns = list(range(nc - 1, -1, -1))

    def turn(j):
        return turns[j // halves]

    def rows_of(j):
        return at((after(turn(j)) * halves + j % halves) * SPAN, SPAN)

    def acopy(j):
        rows = rows_of(j)
        return copy(part.at[1 - core, :, rows], recva.at[:, rows], gs.at[j], gr.at[j], to_core)

    def bcopy(j):
        rows = rows_of(j)
        return copy(sendx.at[rows], recvx.at[rows], hs.at[j], hr.at[j], to_x)

    def backcopy(j):
        landing = at((me * halves + j % halves) * SPAN, SPAN)
        return copy(
            sumc.at[rows_of(j)], back.at[landing], bs.at[j], br.at[j], {"curve": after(turn(j))}
        )

    def cross(j):
        acopy(j).wait_recv()
        rows = rows_of(j)
        sendx[rows, :] = (
            part[core, 1 - xx, rows, :].astype(F32) + recva[1 - xx, rows, :].astype(F32)
        ).astype(BF16)
        bcopy(j).start()

    def home(j):
        bcopy(j).wait_recv()
        rows = rows_of(j)
        total = (
            part[core, xx, rows, :].astype(F32)
            + recva[xx, rows, :].astype(F32)
            + recvx[rows, :].astype(F32)
        ).astype(BF16)
        if turn(j):
            sumc[rows, :] = total
            backcopy(j).start()
        else:
            back[rows, :] = total

    for step in range(chunks + 3):
        if step < chunks:
            attend(after(turn(step)) * halves + step % halves)
            acopy(step).start()
        if 1 <= step <= chunks:
            cross(step - 1)
        if 3 <= step:
            home(step - 3)
    for j in range(chunks - halves):
        backcopy(j).wait_recv()
    total = jnp.zeros((count, 128), F32)
    for t in range(nc):
        total = total + mm(tt[t], back[t * slots : (t + 1) * slots, :])
    out[...] = total.astype(BF16)

    for k in range(nc):
        xcopy(k).wait_send()
        pcopy(k).wait_send()
        fcopy(k).wait_send()
        if k:
            zcopy(k).wait_send()
            ccopy(k).wait_send()
            scopy(k).wait_send()
            dcopy(k).wait_send()
    for j in range(chunks):
        acopy(j).wait_send()
        bcopy(j).wait_send()
        if turn(j):
            backcopy(j).wait_send()


def fused_device(
    points, owner, local_order, codes, w_in, w_bc, decay_rate, dt_scale, skip_gain, w_out
):
    nc = lax.axis_size("curve")
    n_model = lax.axis_size("mp")
    count, width = points.shape
    rows = 2 * count
    slots = rows // nc
    halves = slots // SPAN
    chunks = nc * halves
    cut = HEADS // n_model * HEADDIM
    vm = pltpu.VMEM
    sem = pltpu.SemaphoreType.DMA
    vspec = pl.BlockSpec(memory_space=pltpu.VMEM)
    hbm = pl.BlockSpec(memory_space=pl.ANY)
    sspec = pl.BlockSpec(memory_space=pltpu.SMEM)
    return pl.pallas_call(
        functools.partial(layer_kernel, nc, slots),
        out_shape=jax.ShapeDtypeStruct((count, width // 4), BF16),
        in_specs=[vspec] * 4 + [hbm, vspec] + [sspec] * 3 + [hbm],
        out_specs=vspec,
        scratch_shapes=[
            vm((width, 6 * cut), BF16),
            vm((2, cut, width), BF16),
            sem((2,)),
            vm((nc, slots // 4, width), BF16),
            vm((nc, count, slots), BF16),
            vm((nc, halves, 8, SPAN), F32),
            vm((nc, halves, 8, SPAN), F32),
            vm((rows, width), BF16),
            vm((rows, 6 * cut), BF16),
            vm((2, rows, 128), F32),
            vm((2, rows, 256), F32),
            vm((chunks, 8, 256), F32),
            vm((2, chunks, 64, 256), F32),
            vm((2, chunks, 64, 256), F32),
            vm((2, chunks, 8, 256), F32),
            vm((2, 64, 256), BF16),
            vm((nc, 64, 256), BF16),
            vm((8, 256), F32),
            vm((nc, 8, 256), F32),
            vm((2, 64, 256), F32),
            vm((2, 2, rows, 128), BF16),
            vm((2, rows, 128), BF16),
            vm((rows, 128), BF16),
            vm((rows, 128), BF16),
            vm((rows, 128), BF16),
            vm((rows, 128), BF16),
        ]
        + [sem((nc,))] * 14
        + [sem((chunks,))] * 6,
        compiler_params=pltpu.CompilerParams(
            collective_id=0, has_side_effects=True, vmem_limit_bytes=56 * 1024 * 1024
        ),
    )(
        points,
        owner.reshape(1, count),
        local_order,
        codes.reshape(1, count),
        w_in.reshape(width, 4 * cut),
        w_bc.reshape(width, 256),
        decay_rate,
        dt_scale,
        skip_gain,
        w_out,
    )


def solution(mesh):
    placed = (
        P(("groups", "curve"), None),
        P(("groups", "curve"), None),
        P(("groups", "curve"), None),
        P(("groups", "curve")),
        P(None, None, "mp"),
        P(),
        P(),
        P(),
        P(),
        P(),
    )
    sizes = dict(mesh.shape)

    def body(points, *rest):
        slots = 2 * points.shape[0] // sizes["curve"]
        if sizes["mp"] == 4 and slots % SPAN == 0 and sizes["curve"] <= 8:
            return fused_device(points, *rest)
        return per_device(points, *rest)

    return jax.shard_map(
        body,
        mesh=mesh,
        in_specs=placed,
        out_specs=P(("groups", "curve"), "mp"),
        check_vma=False,
    )
```
